256 devices in a mesh: orb: 32 (over x, z_hi, core), grid: 8 (over y, z_lo).
Axes of the slice: x: 4, y: 4, z: 8 (z_hi: 4, z_lo: 2; z = z_hi * 2 + z_lo), core: 2. Of those that a mesh axis runs over, the one named last changes fastest.
Arguments:
- prior: float32 [384, 32, 48, 128], P('orb', 'grid'), may hold values from -6 to 6
- block: float32 [128, 32, 48, 128], P('orb', 'grid'), may hold values from -36 to 36
- potential: float32 [32, 48, 128], P('grid'), may hold values from -1 to 1
- step_len: float32 [128], P('orb'), may hold values from 0.05 to 0.25
Outputs:
- hprior: float32 [384, 32, 48, 128], P('orb', 'grid')
- hblock: float32 [128, 32, 48, 128], P('orb', 'grid')
- ortho: float32 [128, 32, 48, 128], P('orb', 'grid')
The draws below stay inside these ranges and needn't reach their ends.
All inputs are finite; a program needn't handle non-finite values.
Results may differ from the reference program's by a relative error of at most 0.00012.
Values sent between devices are 32-bit elements; how exact they have to be, the bound alone decides.
No kernel may reach another device: no remote copies, remote signals or barrier semaphores. Data moves between devices by JAX's collectives and lax.ppermute only.
A program may use at most 128 MiB of HBM per device.

```python
import math
import jax
import jax.numpy as jnp
from jax import lax

NX = 48
NY = 128
NPRIOR = 384
NBLK = 128
NZ = 32


def draw_block(key, part):
    key = jax.random.fold_in(key, 7)
    base = jnp.clip(jax.random.normal(key, (NBLK, NZ, NX, NY), jnp.float32), -4.0, 4.0)
    zpos = jnp.arange(NZ, dtype=jnp.float32) / max(NZ - 1, 1)
    xpos = jnp.arange(NX, dtype=jnp.float32) / max(NX - 1, 1)
    amplitude = (1.0 + 2.0 * zpos)[:, None, None] * (1.0 + 2.0 * xpos)[None, :, None]
    return base * amplitude[None]


def shard_levels(stream_key, shape, shards, low, largest):
    factor_of, own = 1.0, jax.random.fold_in(stream_key, 6)
    for dim, blocks in shards:
        draws = jnp.exp(jax.random.uniform(jax.random.fold_in(own, dim), (blocks,), jnp.float32, low / len(shards), largest / len(shards)))
        factor_of = factor_of * jnp.repeat(draws, shape[dim] // blocks).reshape([-1 if axis == dim else 1 for axis in range(len(shape))])
    return factor_of


def gaussian(rng, shape, scale, reach, shards=(), kind=jnp.bfloat16):
    result = jax.random.normal(rng, shape, jnp.float32) * scale
    if len(shards) > 0:
        result = shard_levels(rng, shape, shards, -0.22, 0.18) * result
    return jnp.clip(result, min=-reach, max=reach).astype(kind)


def setup_inputs(seed: int = 0) -> dict:
    seeds = jax.random.split(jax.random.key(seed), 5)
    return {
        "prior": gaussian(seeds[0], (NPRIOR, NZ, NX, NY), 1.0, 6.0, ((0, 32), (1, 8)), jnp.float32),
        "block": draw_block(jax.random.fold_in(seeds[4], 71), 0),
        "potential": jnp.clip(jax.random.uniform(seeds[2], (NZ, NX, NY), jnp.float32, -1.0, 1.0) * shard_levels(seeds[2], (NZ, NX, NY), ((0, 8),), -0.4, 0.0), -1.0, 1.0),
        "step_len": jnp.clip(jnp.exp(math.log(0.25) - 1.609438 * jax.random.uniform(seeds[3], (NBLK,), jnp.float32) ** shard_levels(seeds[3], (NBLK,), ((0, 32),), -0.2, 0.2)), 0.05, 0.25),
    }


near_coef = 4.0 / 3.0
far_coef = -1.0 / 12.0
norm_eps = 1e-06

def hamiltonian(field, potential):
    total = -7.5 * field
    for axis_num in (0, 1, 2):
        total = total + near_coef * (jnp.roll(field, 1, axis_num) + jnp.roll(field, -1, axis_num))
        total = total + far_coef * (jnp.roll(field, 2, axis_num) + jnp.roll(field, -2, axis_num))
    return -0.5 * total + potential * field

def apply_all(fields, potential):

    def single(field):
        return hamiltonian(field, potential)
    return lax.map(single, fields)

def reference(prior, block, potential, step_len):
    hprior = apply_all(prior, potential)
    hblock = apply_all(block, potential)
    trial = block - step_len[:, None, None, None] * hblock
    ncells = NX * NY * NZ
    flat_prior = prior.reshape(NPRIOR, -1)
    flat_trial = trial.reshape(NBLK, -1)
    coeff = lax.dot_general(flat_prior, flat_trial, (((1,), (1,)), ((), ())), precision=lax.Precision.HIGHEST, preferred_element_type=jnp.float32) / ncells
    correction = lax.dot_general(coeff, flat_prior, (((0,), (0,)), ((), ())), precision=lax.Precision.HIGHEST, preferred_element_type=jnp.float32)
    proj = flat_trial - correction
    sqnorm = lax.optimization_barrier(jnp.sum(proj * proj, axis=1)) / ncells
    ortho = proj * lax.rsqrt(sqnorm + norm_eps)[:, None]
    return (hprior, hblock, ortho.reshape(NBLK, NZ, NX, NY))
```

```python
import jax
import jax.numpy as jnp
from jax import lax
from jax.experimental import pallas as pl
from jax.experimental.pallas import tpu as pltpu
from jax.sharding import Mesh, PartitionSpec as P

NORM_EPS = 1e-06
ORB = ("x", "zh", "core")
GRID = ("y", "zl")
NORB = 32
NGRID = 8
LANES = 128
HIGHEST = lax.Precision.HIGHEST
VMEM = pl.BlockSpec(memory_space=pltpu.VMEM)
SMEM = pl.BlockSpec(memory_space=pltpu.SMEM)
PARAMS = pltpu.CompilerParams(vmem_limit_bytes=32 * 1024 * 1024)


def call(kernel, out_shape, in_specs, flops, nbytes):
    single = isinstance(out_shape[0], int)
    shapes = [out_shape] if single else list(out_shape)
    outs = pl.pallas_call(
        kernel,
        out_shape=[jax.ShapeDtypeStruct(s, jnp.float32) for s in shapes],
        in_specs=in_specs,
        out_specs=[VMEM] * len(shapes),
        compiler_params=PARAMS,
        cost_estimate=pl.CostEstimate(flops=flops, bytes_accessed=nbytes, transcendentals=0),
    )
    return (lambda *a: outs(*a)[0]) if single else outs


def apply_stencil(layer, below, above, pot):
    near = below[0] + above[0]
    far = below[1] + above[1]
    rows = layer.shape[0]
    near = near + (pltpu.roll(layer, 1, 0) + pltpu.roll(layer, rows - 1, 0))
    far = far + (pltpu.roll(layer, 2, 0) + pltpu.roll(layer, rows - 2, 0))
    near = near + (pltpu.roll(layer, 1, 1) + pltpu.roll(layer, LANES - 1, 1))
    far = far + (pltpu.roll(layer, 2, 1) + pltpu.roll(layer, LANES - 2, 1))
    return (3.75 + pot) * layer - (2.0 / 3.0) * near + (1.0 / 24.0) * far


def orbital_layers(field_ref, low_ref, high_ref, n):
    layers = [low_ref[n, 0], low_ref[n, 1]]
    layers += [field_ref[n, z] for z in range(field_ref.shape[1])]
    layers += [high_ref[n, 0], high_ref[n, 1]]
    return layers


def stencil_layers(layers, pot_ref):
    for z in range(len(layers) - 4):
        c = z + 2
        yield z, apply_stencil(
            layers[c], (layers[c - 1], layers[c - 2]), (layers[c + 1], layers[c + 2]), pot_ref[z]
        )


def prior_kernel(field_ref, low_ref, high_ref, pot_ref, out_ref):
    def step(n, carry):
        layers = orbital_layers(field_ref, low_ref, high_ref, n)
        for z, value in stencil_layers(layers, pot_ref):
            out_ref[n, z] = value
        return carry

    lax.fori_loop(0, field_ref.shape[0], step, 0)


def block_kernel(field_ref, low_ref, high_ref, pot_ref, step_ref, out_ref, packed_ref):
    nz, nx = field_ref.shape[1], field_ref.shape[2]
    rows = nz * nx // NORB
    per_layer = nx // rows
    for n in range(field_ref.shape[0]):
        layers = orbital_layers(field_ref, low_ref, high_ref, n)
        for z, value in stencil_layers(layers, pot_ref):
            out_ref[n, z] = value
            trial = layers[z + 2] - step_ref[n] * value
            for part in range(per_layer):
                packed_ref[z * per_layer + part, n * rows : (n + 1) * rows, :] = trial[
                    part * rows : (part + 1) * rows
                ]


def pack_kernel(field_ref, packed_ref):
    count, total, _ = field_ref.shape
    rows = total // NORB
    for n in range(count):
        for dest in range(NORB):
            packed_ref[dest, n * rows : (n + 1) * rows, :] = field_ref[
                n, dest * rows : (dest + 1) * rows, :
            ]


def make_coef_kernel(nprior, nblk, rows):
    def kernel(prior_ref, trial_ref, out_ref):
        total = jnp.zeros((nprior, nblk), jnp.float32)
        for r in range(rows):
            left = prior_ref[pl.ds(r, nprior, stride=rows), :]
            right = trial_ref[pl.ds(r, nblk, stride=rows), :]
            total += lax.dot_general(
                left, right, (((1,), (1,)), ((), ())),
                precision=HIGHEST, preferred_element_type=jnp.float32,
            )
        out_ref[...] = total

    return kernel


def make_proj_kernel(nprior, nblk, rows):
    def kernel(coef_ref, prior_ref, trial_ref, out_ref):
        coef_t = coef_ref[...].T
        for r in range(rows):
            left = prior_ref[pl.ds(r, nprior, stride=rows), :]
            removed = jnp.dot(
                coef_t, left, precision=HIGHEST, preferred_element_type=jnp.float32
            )
            out_ref[pl.ds(r, nblk, stride=rows), :] = (
                trial_ref[pl.ds(r, nblk, stride=rows), :] - removed
            )

    return kernel


def square_kernel(proj_ref, out_ref):
    count = 4
    rows = proj_ref.shape[1] // count
    value = proj_ref[0]
    total = value * value
    for s in range(1, proj_ref.shape[0]):
        value = proj_ref[s]
        total = total + value * value
    out_ref[...] = jnp.zeros_like(out_ref)
    for n in range(count):
        out_ref[n : n + 1, :] = jnp.sum(total[n * rows : (n + 1) * rows], axis=0, keepdims=True)


def make_scale_kernel(ncells):
    def kernel(proj_ref, parts_ref, out_ref):
        count = out_ref.shape[0]
        rows = proj_ref.shape[1] // count
        total = parts_ref[0]
        for s in range(1, parts_ref.shape[0]):
            total = total + parts_ref[s]
        sqnorm = jnp.sum(total, axis=1, keepdims=True) / ncells
        scale = lax.rsqrt(sqnorm + NORM_EPS)
        for n in range(count):
            factor = jnp.broadcast_to(scale[n : n + 1], (rows, LANES))
            for s in range(proj_ref.shape[0]):
                out_ref[n, s * rows : (s + 1) * rows, :] = (
                    proj_ref[s, n * rows : (n + 1) * rows, :] * factor
                )

    return kernel


def exchange(value, axes):
    return lax.all_to_all(value, axes, 0, 0, tiled=True)


def spread(value, axes, count):
    return exchange(jnp.broadcast_to(value[None], (count,) + value.shape), axes)


def halos(fields):
    forward = [(i, (i + 1) % NGRID) for i in range(NGRID)]
    backward = [(target, source) for source, target in forward]
    low = lax.ppermute(fields[:, -2:], GRID, forward)
    high = lax.ppermute(fields[:, :2], GRID, backward)
    return low, high


def on_device(prior, block, potential, step_len):
    nprior_loc, nz, nx, ny = prior.shape
    nblk_loc = block.shape[0]
    nprior, nblk = nprior_loc * NORB, nblk_loc * NORB
    cells = nz * nx * ny
    ncells = cells * NGRID
    rows = nz * nx // NORB
    size = 4 * cells

    packed = call(
        pack_kernel, (NORB, nprior_loc * rows, LANES), [VMEM], 0, 2 * nprior_loc * size
    )(prior.reshape(nprior_loc, nz * nx, ny))

    blow, bhigh = halos(block)
    plow, phigh = halos(prior)
    prior_cells = exchange(packed, ORB).reshape(nprior * rows, LANES)

    hblock, trial = call(
        block_kernel,
        [block.shape, (NORB, nblk_loc * rows, LANES)],
        [VMEM, VMEM, VMEM, VMEM, SMEM],
        20 * nblk_loc * cells,
        4 * nblk_loc * size,
    )(block, blow, bhigh, potential, step_len)
    trial_cells = exchange(trial, ORB).reshape(nblk * rows, LANES)

    hprior = call(
        prior_kernel, prior.shape, [VMEM] * 4, 20 * nprior_loc * cells, 3 * nprior_loc * size
    )(prior, plow, phigh, potential)

    coef_bytes = 4 * nprior * nblk
    gemm = 2 * nprior * nblk * rows * LANES
    partial = call(
        make_coef_kernel(nprior, nblk, rows), (nprior, nblk), [VMEM] * 2, gemm, 4 * coef_bytes
    )(prior_cells, trial_cells)
    first = 16
    share = exchange(partial.reshape(first, nprior // first, nblk), ("x", "y"))
    share = jnp.sum(share, axis=0)
    share = jnp.sum(spread(share, ("zh", "core", "zl"), 16), axis=0) / ncells
    coeff = spread(share, ("x", "y"), first).reshape(nprior, nblk)

    proj = call(
        make_proj_kernel(nprior, nblk, rows),
        (nblk * rows, LANES),
        [VMEM] * 3,
        gemm,
        6 * coef_bytes,
    )(coeff, prior_cells, trial_cells)
    back = exchange(proj.reshape(NORB, nblk_loc * rows, LANES), ORB)
    squares = call(square_kernel, (8, LANES), [VMEM], 2 * nblk_loc * cells, nblk_loc * size)(back)
    parts = spread(squares, GRID, NGRID)
    ortho = call(
        make_scale_kernel(ncells),
        (nblk_loc, nz * nx, ny),
        [VMEM] * 2,
        nblk_loc * cells,
        2 * nblk_loc * size,
    )(back, parts)
    return hprior, hblock, ortho.reshape(block.shape)


def solution(mesh):
    fine = Mesh(mesh.devices.reshape(4, 4, 2, 4, 2), ORB + GRID)
    fields = P(ORB, GRID, None, None)
    in_specs = (fields, fields, P(GRID, None, None), P(ORB))
    return jax.shard_map(
        on_device, mesh=fine, in_specs=in_specs, out_specs=(fields,) * 3, check_vma=False
    )
```

```python
import jax
import jax.numpy as jnp
from jax import lax
from jax.experimental import pallas as pl
from jax.experimental.pallas import tpu as pltpu
from jax.sharding import Mesh, PartitionSpec as P

NORM_EPS = 1e-06
NEAR = 2.0 / 3.0
FAR = 1.0 / 24.0
ORB = ("x", "zh", "core")
GRID = ("y", "zl")
NORB = 32
NGRID = 8
LANES = 128
FORWARD = [(i, (i + 1) % NGRID) for i in range(NGRID)]
BACKWARD = [(target, source) for source, target in FORWARD]
HIGHEST = lax.Precision.HIGHEST
VMEM = pl.BlockSpec(memory_space=pltpu.VMEM)
SMEM = pl.BlockSpec(memory_space=pltpu.SMEM)
PARAMS = pltpu.CompilerParams(vmem_limit_bytes=16 * 1024 * 1024)


def call(kernel, out_shape, in_specs, flops, nbytes):
    single = isinstance(out_shape[0], int)
    shapes = [out_shape] if single else list(out_shape)
    outs = pl.pallas_call(
        kernel,
        out_shape=[jax.ShapeDtypeStruct(s, jnp.float32) for s in shapes],
        in_specs=in_specs,
        out_specs=[VMEM] * len(shapes),
        compiler_params=PARAMS,
        cost_estimate=pl.CostEstimate(flops=flops, bytes_accessed=nbytes, transcendentals=0),
    )
    return (lambda *a: outs(*a)[0]) if single else outs


def apply_stencil(layer, below, above, pot):
    near = below[0] + above[0]
    far = below[1] + above[1]
    rows = layer.shape[0]
    near = near + (pltpu.roll(layer, 1, 0) + pltpu.roll(layer, rows - 1, 0))
    far = far + (pltpu.roll(layer, 2, 0) + pltpu.roll(layer, rows - 2, 0))
    near = near + (pltpu.roll(layer, 1, 1) + pltpu.roll(layer, LANES - 1, 1))
    far = far + (pltpu.roll(layer, 2, 1) + pltpu.roll(layer, LANES - 2, 1))
    return (3.75 + pot) * layer - NEAR * near + FAR * far


def orbital_layers(field_ref, low_ref, high_ref, n):
    layers = [low_ref[n, 0], low_ref[n, 1]]
    layers += [field_ref[n, z] for z in range(field_ref.shape[1])]
    layers += [high_ref[n, 0], high_ref[n, 1]]
    return layers


def stencil_layers(layers, pot_ref):
    for z in range(len(layers) - 4):
        c = z + 2
        yield z, apply_stencil(
            layers[c], (layers[c - 1], layers[c - 2]), (layers[c + 1], layers[c + 2]), pot_ref[z]
        )


def prior_kernel(field_ref, low_ref, high_ref, pot_ref, out_ref):
    def step(n, carry):
        layers = orbital_layers(field_ref, low_ref, high_ref, n)
        for z, value in stencil_layers(layers, pot_ref):
            out_ref[n, z] = value
        return carry

    lax.fori_loop(0, field_ref.shape[0], step, 0)


def put(packed_ref, slot, z, layer, nz):
    rows = nz * layer.shape[0] // NORB
    per_layer = NORB // nz
    for part in range(per_layer):
        packed_ref[z * per_layer + part, slot * rows : (slot + 1) * rows, :] = layer[
            part * rows : (part + 1) * rows
        ]


def inner_kernel(prior_ref, field_ref, pot_ref, step_ref, packed_ref, copy_ref, inner_ref, steps_ref):
    nprior, nz, nx, _ = prior_ref.shape
    nblk = field_ref.shape[0]
    for n in range(nprior):
        for z in range(nz):
            put(packed_ref, n, z, prior_ref[n, z], nz)
    zero = jnp.zeros((nx, LANES), jnp.float32)
    for n in range(nblk):
        layers = [zero, zero] + [field_ref[n, z] for z in range(nz)] + [zero, zero]
        for z, value in stencil_layers(layers, pot_ref):
            inner_ref[n, z] = value
            copy_ref[n, z] = layers[z + 2]
        steps_ref[n] = jnp.full((8, LANES), step_ref[n], jnp.float32)


def outer_kernel(prior_ref, field_ref, inner_ref, steps_ref, low_ref, high_ref, out_ref, packed_ref):
    nblk, nz, nx, _ = field_ref.shape
    rows = nz * nx // NORB
    nprior = prior_ref.shape[1] // rows
    for dest in range(NORB):
        packed_ref[dest, : nprior * rows, :] = prior_ref[dest]
    for n in range(nblk):
        edge = {
            0: FAR * low_ref[n, 0] - NEAR * low_ref[n, 1],
            1: FAR * low_ref[n, 1],
            nz - 2: FAR * high_ref[n, 0],
            nz - 1: FAR * high_ref[n, 1] - NEAR * high_ref[n, 0],
        }
        step = jnp.broadcast_to(steps_ref[n, 0:1], (nx, LANES))
        for z in range(nz):
            value = inner_ref[n, z] + edge[z]
            out_ref[n, z] = value
            put(packed_ref, nprior + n, z, field_ref[n, z] - step * value, nz)


def make_coef_kernel(nprior, nblk, rows):
    count, split = nprior // NORB * rows, nblk // NORB * rows

    def kernel(cells_ref, out_ref, prior_ref, trial_ref):
        for s in range(NORB):
            prior_ref[s * count : (s + 1) * count, :] = cells_ref[s, :count, :]
            trial_ref[s * split : (s + 1) * split, :] = cells_ref[s, count:, :]
        total = jnp.zeros((nprior, nblk), jnp.float32)
        for r in range(rows):
            left = prior_ref[pl.ds(r, nprior, stride=rows), :]
            right = trial_ref[pl.ds(r, nblk, stride=rows), :]
            total += lax.dot_general(
                left, right, (((1,), (1,)), ((), ())),
                precision=HIGHEST, preferred_element_type=jnp.float32,
            )
        out_ref[...] = total

    return kernel


def make_proj_kernel(nprior, nblk, rows):
    def kernel(coef_ref, prior_ref, trial_ref, out_ref):
        coef_t = coef_ref[...].T
        for r in range(rows):
            left = prior_ref[pl.ds(r, nprior, stride=rows), :]
            removed = jnp.dot(
                coef_t, left, precision=HIGHEST, preferred_element_type=jnp.float32
            )
            out_ref[pl.ds(r, nblk, stride=rows), :] = (
                trial_ref[pl.ds(r, nblk, stride=rows), :] - removed
            )

    return kernel


def square_kernel(proj_ref, out_ref):
    count = 4
    rows = proj_ref.shape[1] // count
    value = proj_ref[0]
    total = value * value
    for s in range(1, proj_ref.shape[0]):
        value = proj_ref[s]
        total = total + value * value
    out_ref[...] = jnp.zeros_like(out_ref)
    for n in range(count):
        out_ref[n : n + 1, :] = jnp.sum(total[n * rows : (n + 1) * rows], axis=0, keepdims=True)


def make_scale_kernel(ncells):
    def kernel(proj_ref, parts_ref, out_ref):
        count = out_ref.shape[0]
        rows = proj_ref.shape[1] // count
        total = parts_ref[0]
        for s in range(1, parts_ref.shape[0]):
            total = total + parts_ref[s]
        sqnorm = jnp.sum(total, axis=1, keepdims=True) / ncells
        scale = lax.rsqrt(sqnorm + NORM_EPS)
        for n in range(count):
            factor = jnp.broadcast_to(scale[n : n + 1], (rows, LANES))
            for s in range(proj_ref.shape[0]):
                out_ref[n, s * rows : (s + 1) * rows, :] = (
                    proj_ref[s, n * rows : (n + 1) * rows, :] * factor
                )

    return kernel


def exchange(value, axes):
    return lax.all_to_all(value, axes, 0, 0, tiled=True)


def repeat(value, count):
    return jnp.broadcast_to(value[None], (count,) + value.shape)


def edges(fields):
    return fields[:, -2:], fields[:, :2]


def halos(sides):
    return lax.ppermute(sides[0], GRID, FORWARD), lax.ppermute(sides[1], GRID, BACKWARD)


def on_device(prior, block, potential, step_len):
    nprior_loc, nz, nx, ny = prior.shape
    nblk_loc = block.shape[0]
    nprior, nblk = nprior_loc * NORB, nblk_loc * NORB
    cells = nz * nx * ny
    ncells = cells * NGRID
    rows = nz * nx // NORB
    size = 4 * cells

    blow, bhigh = halos(edges(block))
    prior_rows, field, inner, steps = call(
        inner_kernel,
        [
            (NORB, nprior_loc * rows, LANES),
            block.shape,
            block.shape,
            (nblk_loc, 8, LANES),
        ],
        [VMEM] * 3 + [SMEM],
        20 * nblk_loc * cells,
        (2 * nprior_loc + 4 * nblk_loc) * size,
    )(prior, block, potential, step_len)
    hblock, packed = call(
        outer_kernel,
        [block.shape, (NORB, (nprior_loc + nblk_loc) * rows, LANES)],
        [VMEM] * 6,
        4 * nblk_loc * cells,
        (2 * nprior_loc + 4 * nblk_loc) * size,
    )(prior_rows, field, inner, steps, blow, bhigh)
    moved = exchange(packed, ORB)

    low_edge, high_edge = edges(prior)
    moved, low_edge, high_edge = lax.optimization_barrier((moved, low_edge, high_edge))
    coef_bytes = 4 * nprior * nblk
    gemm = 2 * nprior * nblk * rows * LANES
    partial, prior_cells, trial_cells = call(
        make_coef_kernel(nprior, nblk, rows),
        [(nprior, nblk), (nprior * rows, LANES), (nblk * rows, LANES)],
        [VMEM],
        gemm,
        16 * coef_bytes,
    )(moved)
    first = 16
    share = jnp.sum(exchange(partial.reshape(first, nprior // first, nblk), ("x", "y")), axis=0)
    phigh = lax.ppermute(high_edge, GRID, BACKWARD)
    share, low_edge, phigh = lax.optimization_barrier((share, low_edge, phigh))
    plow = lax.ppermute(low_edge, GRID, FORWARD)
    share = jnp.sum(exchange(repeat(share, 16), ("zh", "core", "zl")), axis=0) / ncells
    coeff = exchange(repeat(share, first), ("x", "y")).reshape(nprior, nblk)
    coeff, plow = lax.optimization_barrier((coeff, plow))

    proj = call(
        make_proj_kernel(nprior, nblk, rows),
        (nblk * rows, LANES),
        [VMEM] * 3,
        gemm,
        6 * coef_bytes,
    )(coeff, prior_cells, trial_cells)
    back = exchange(proj.reshape(NORB, nblk_loc * rows, LANES), ORB)
    hprior = call(
        prior_kernel, prior.shape, [VMEM] * 4, 20 * nprior_loc * cells, 3 * nprior_loc * size
    )(prior, plow, phigh, potential)
    squares = call(square_kernel, (8, LANES), [VMEM], 2 * nblk_loc * cells, nblk_loc * size)(back)
    totals = exchange(repeat(squares, NGRID), GRID)
    ortho = call(
        make_scale_kernel(ncells),
        (nblk_loc, nz * nx, ny),
        [VMEM] * 2,
        nblk_loc * cells,
        2 * nblk_loc * size,
    )(back, totals)
    return hprior, hblock, ortho.reshape(block.shape)


def solution(mesh):
    fine = Mesh(mesh.devices.reshape(4, 4, 2, 4, 2), ORB + GRID)
    fields = P(ORB, GRID, None, None)
    in_specs = (fields, fields, P(GRID, None, None), P(ORB))
    return jax.shard_map(
        on_device, mesh=fine, in_specs=in_specs, out_specs=(fields,) * 3, check_vma=False
    )
```

```python
import jax
import jax.numpy as jnp
from jax import lax
from jax.experimental import pallas as pl
from jax.experimental.pallas import tpu as pltpu
from jax.sharding import Mesh, PartitionSpec as P

NORM_EPS = 1e-06
NEAR = 2.0 / 3.0
FAR = 1.0 / 24.0
ORB = ("x", "zh", "core")
GRID = ("y", "zl")
NORB = 32
NGRID = 8
LANES = 128
FORWARD = [(i, (i + 1) % NGRID) for i in range(NGRID)]
BACKWARD = [(target, source) for source, target in FORWARD]
SWAP = [(0, 1), (1, 0)]
ALONG = [(i, (i + (NGRID - 2 if i % 2 else 2)) % NGRID) for i in range(NGRID)]
HIGHEST = lax.Precision.HIGHEST
VMEM = pl.BlockSpec(memory_space=pltpu.VMEM)
SMEM = pl.BlockSpec(memory_space=pltpu.SMEM)
PARAMS = pltpu.CompilerParams(vmem_limit_bytes=16 * 1024 * 1024)


def call(kernel, out_shape, in_specs, flops, nbytes):
    single = isinstance(out_shape[0], int)
    shapes = [out_shape] if single else list(out_shape)
    outs = pl.pallas_call(
        kernel,
        out_shape=[jax.ShapeDtypeStruct(s, jnp.float32) for s in shapes],
        in_specs=in_specs,
        out_specs=[VMEM] * len(shapes),
        compiler_params=PARAMS,
        cost_estimate=pl.CostEstimate(flops=flops, bytes_accessed=nbytes, transcendentals=0),
    )
    return (lambda *a: outs(*a)[0]) if single else outs


def apply_stencil(layer, below, above, pot):
    near = below[0] + above[0]
    far = below[1] + above[1]
    rows = layer.shape[0]
    near = near + (pltpu.roll(layer, 1, 0) + pltpu.roll(layer, rows - 1, 0))
    far = far + (pltpu.roll(layer, 2, 0) + pltpu.roll(layer, rows - 2, 0))
    near = near + (pltpu.roll(layer, 1, 1) + pltpu.roll(layer, LANES - 1, 1))
    far = far + (pltpu.roll(layer, 2, 1) + pltpu.roll(layer, LANES - 2, 1))
    return (3.75 + pot) * layer - NEAR * near + FAR * far


def stencil_layers(layers, pot_ref):
    for z in range(len(layers) - 4):
        c = z + 2
        yield z, apply_stencil(
            layers[c], (layers[c - 1], layers[c - 2]), (layers[c + 1], layers[c + 2]), pot_ref[z]
        )


def prior_kernel(field_ref, near_ref, wrapped_ref, pot_ref, out_ref):
    upper = lax.axis_index("zl") == 1

    def step(n, carry):
        near = [near_ref[n, z] for z in range(2)]
        wrapped = [wrapped_ref[n, z] for z in range(2)]
        low = [jnp.where(upper, near[z], wrapped[z]) for z in range(2)]
        high = [jnp.where(upper, wrapped[z], near[z]) for z in range(2)]
        layers = low + [field_ref[n, z] for z in range(field_ref.shape[1])] + high
        for z, value in stencil_layers(layers, pot_ref):
            out_ref[n, z] = value
        return carry

    lax.fori_loop(0, field_ref.shape[0], step, 0)


def put(packed_ref, slot, z, layer, nz):
    rows = nz * layer.shape[0] // NORB
    per_layer = NORB // nz
    for part in range(per_layer):
        packed_ref[z * per_layer + part, slot * rows : (slot + 1) * rows, :] = layer[
            part * rows : (part + 1) * rows
        ]


def inner_kernel(
    prior_ref, field_ref, pot_ref, step_ref,
    packed_ref, near_ref, far_ref, copy_ref, inner_ref, steps_ref,
):
    nprior, nz, nx, _ = prior_ref.shape
    nblk = field_ref.shape[0]
    upper = lax.axis_index("zl") == 1
    for n in range(nprior):
        for z in range(nz):
            put(packed_ref, n, z, prior_ref[n, z], nz)
        for z in range(2):
            top, bottom = prior_ref[n, nz - 2 + z], prior_ref[n, z]
            near_ref[n, z] = jnp.where(upper, bottom, top)
            far_ref[n, z] = jnp.where(upper, top, bottom)
    zero = jnp.zeros((nx, LANES), jnp.float32)
    for n in range(nblk):
        layers = [zero, zero] + [field_ref[n, z] for z in range(nz)] + [zero, zero]
        for z, value in stencil_layers(layers, pot_ref):
            inner_ref[n, z] = value
            copy_ref[n, z] = layers[z + 2]
        steps_ref[n] = jnp.full((8, LANES), step_ref[n], jnp.float32)


def outer_kernel(prior_ref, field_ref, inner_ref, steps_ref, low_ref, high_ref, out_ref, packed_ref):
    nblk, nz, nx, _ = field_ref.shape
    rows = nz * nx // NORB
    nprior = prior_ref.shape[1] // rows
    for dest in range(NORB):
        packed_ref[dest, : nprior * rows, :] = prior_ref[dest]
    for n in range(nblk):
        edge = {
            0: FAR * low_ref[n, 0] - NEAR * low_ref[n, 1],
            1: FAR * low_ref[n, 1],
            nz - 2: FAR * high_ref[n, 0],
            nz - 1: FAR * high_ref[n, 1] - NEAR * high_ref[n, 0],
        }
        step = jnp.broadcast_to(steps_ref[n, 0:1], (nx, LANES))
        for z in range(nz):
            value = inner_ref[n, z] + edge[z]
            out_ref[n, z] = value
            put(packed_ref, nprior + n, z, field_ref[n, z] - step * value, nz)


def make_coef_kernel(nprior, nblk, rows):
    count, split = nprior // NORB * rows, nblk // NORB * rows

    def kernel(cells_ref, out_ref, prior_ref, trial_ref):
        for s in range(NORB):
            prior_ref[s * count : (s + 1) * count, :] = cells_ref[s, :count, :]
            trial_ref[s * split : (s + 1) * split, :] = cells_ref[s, count:, :]
        total = jnp.zeros((nprior, nblk), jnp.float32)
        for r in range(rows):
            left = prior_ref[pl.ds(r, nprior, stride=rows), :]
            right = trial_ref[pl.ds(r, nblk, stride=rows), :]
            total += lax.dot_general(
                left, right, (((1,), (1,)), ((), ())),
                precision=HIGHEST, preferred_element_type=jnp.float32,
            )
        out_ref[...] = total

    return kernel


def make_proj_kernel(nprior, nblk, rows):
    def kernel(coef_ref, prior_ref, trial_ref, out_ref):
        coef_t = coef_ref[...].T
        for r in range(rows):
            left = prior_ref[pl.ds(r, nprior, stride=rows), :]
            removed = jnp.dot(
                coef_t, left, precision=HIGHEST, preferred_element_type=jnp.float32
            )
            out_ref[pl.ds(r, nblk, stride=rows), :] = (
                trial_ref[pl.ds(r, nblk, stride=rows), :] - removed
            )

    return kernel


def square_kernel(proj_ref, out_ref):
    count = 4
    rows = proj_ref.shape[1] // count
    value = proj_ref[0]
    total = value * value
    for s in range(1, proj_ref.shape[0]):
        value = proj_ref[s]
        total = total + value * value
    out_ref[...] = jnp.zeros_like(out_ref)
    for n in range(count):
        out_ref[n : n + 1, :] = jnp.sum(total[n * rows : (n + 1) * rows], axis=0, keepdims=True)


def make_scale_kernel(ncells):
    def kernel(proj_ref, parts_ref, out_ref):
        count = out_ref.shape[0]
        rows = proj_ref.shape[1] // count
        total = parts_ref[0]
        for s in range(1, parts_ref.shape[0]):
            total = total + parts_ref[s]
        sqnorm = jnp.sum(total, axis=1, keepdims=True) / ncells
        scale = lax.rsqrt(sqnorm + NORM_EPS)
        for n in range(count):
            factor = jnp.broadcast_to(scale[n : n + 1], (rows, LANES))
            for s in range(proj_ref.shape[0]):
                out_ref[n, s * rows : (s + 1) * rows, :] = (
                    proj_ref[s, n * rows : (n + 1) * rows, :] * factor
                )

    return kernel


def exchange(value, axes):
    return lax.all_to_all(value, axes, 0, 0, tiled=True)


def repeat(value, count):
    return jnp.broadcast_to(value[None], (count,) + value.shape)


def edges(fields):
    return fields[:, -2:], fields[:, :2]


def halos(sides):
    return lax.ppermute(sides[0], GRID, FORWARD), lax.ppermute(sides[1], GRID, BACKWARD)


def on_device(prior, block, potential, step_len):
    nprior_loc, nz, nx, ny = prior.shape
    nblk_loc = block.shape[0]
    nprior, nblk = nprior_loc * NORB, nblk_loc * NORB
    cells = nz * nx * ny
    ncells = cells * NGRID
    rows = nz * nx // NORB
    size = 4 * cells

    blow, bhigh = halos(edges(block))
    prior_rows, near, wrapped, field, inner, steps = call(
        inner_kernel,
        [
            (NORB, nprior_loc * rows, LANES),
            (nprior_loc, 2, nx, ny),
            (nprior_loc, 2, nx, ny),
            block.shape,
            block.shape,
            (nblk_loc, 8, LANES),
        ],
        [VMEM] * 3 + [SMEM],
        20 * nblk_loc * cells,
        (2 * nprior_loc + 4 * nblk_loc) * size,
    )(prior, block, potential, step_len)
    hblock, packed = call(
        outer_kernel,
        [block.shape, (NORB, (nprior_loc + nblk_loc) * rows, LANES)],
        [VMEM] * 6,
        4 * nblk_loc * cells,
        (2 * nprior_loc + 4 * nblk_loc) * size,
    )(prior_rows, field, inner, steps, blow, bhigh)
    moved = exchange(packed, ORB)

    moved, near, wrapped = lax.optimization_barrier((moved, near, wrapped))
    coef_bytes = 4 * nprior * nblk
    gemm = 2 * nprior * nblk * rows * LANES
    partial, prior_cells, trial_cells = call(
        make_coef_kernel(nprior, nblk, rows),
        [(nprior, nblk), (nprior * rows, LANES), (nblk * rows, LANES)],
        [VMEM],
        gemm,
        16 * coef_bytes,
    )(moved)
    first = 16
    near = lax.ppermute(near, "zl", SWAP)
    share = jnp.sum(exchange(partial.reshape(first, nprior // first, nblk), ("x", "y")), axis=0)
    share, near = lax.optimization_barrier((share, near))
    share = jnp.sum(exchange(repeat(share, 16), ("zh", "core", "zl")), axis=0) / ncells
    share, wrapped = lax.optimization_barrier((share, wrapped))
    wrapped = lax.ppermute(wrapped, "zl", SWAP)
    coeff = exchange(repeat(share, first), ("x", "y")).reshape(nprior, nblk)

    proj = call(
        make_proj_kernel(nprior, nblk, rows),
        (nblk * rows, LANES),
        [VMEM] * 3,
        gemm,
        6 * coef_bytes,
    )(coeff, prior_cells, trial_cells)
    proj, wrapped = lax.optimization_barrier((proj, wrapped))
    wrapped = lax.ppermute(wrapped, GRID, ALONG)
    back = exchange(proj.reshape(NORB, nblk_loc * rows, LANES), ORB)
    hprior = call(
        prior_kernel, prior.shape, [VMEM] * 4, 20 * nprior_loc * cells, 3 * nprior_loc * size
    )(prior, near, wrapped, potential)
    squares = call(square_kernel, (8, LANES), [VMEM], 2 * nblk_loc * cells, nblk_loc * size)(back)
    totals = exchange(repeat(squares, NGRID), GRID)
    ortho = call(
        make_scale_kernel(ncells),
        (nblk_loc, nz * nx, ny),
        [VMEM] * 2,
        nblk_loc * cells,
        2 * nblk_loc * size,
    )(back, totals)
    return hprior, hblock, ortho.reshape(block.shape)


def solution(mesh):
    fine = Mesh(mesh.devices.reshape(4, 4, 2, 4, 2), ORB + GRID)
    fields = P(ORB, GRID, None, None)
    in_specs = (fields, fields, P(GRID, None, None), P(ORB))
    return jax.shard_map(
        on_device, mesh=fine, in_specs=in_specs, out_specs=(fields,) * 3, check_vma=False
    )
```

```python
import jax
import jax.numpy as jnp
from jax import lax
from jax.experimental import pallas as pl
from jax.experimental.pallas import tpu as pltpu
from jax.sharding import Mesh, PartitionSpec as P

NORM_EPS = 1e-06
NEAR = 2.0 / 3.0
FAR = 1.0 / 24.0
ORB = ("x", "zh", "core")
GRID = ("y", "zl")
NORB = 32
NGRID = 8
LANES = 128
FORWARD = [(i, (i + 1) % NGRID) for i in range(NGRID)]
BACKWARD = [(target, source) for source, target in FORWARD]
SWAP = [(0, 1), (1, 0)]
ALONG = [(i, (i + (NGRID - 2 if i % 2 else 2)) % NGRID) for i in range(NGRID)]
HIGHEST = lax.Precision.HIGHEST
VMEM = pl.BlockSpec(memory_space=pltpu.VMEM)
SMEM = pl.BlockSpec(memory_space=pltpu.SMEM)
PARAMS = pltpu.CompilerParams(vmem_limit_bytes=16 * 1024 * 1024)


def call(kernel, out_shape, in_specs, flops, nbytes, pin=False, scratch=()):
    single = isinstance(out_shape[0], int)
    shapes = [out_shape] if single else list(out_shape)
    outs = pl.pallas_call(
        kernel,
        out_shape=[
            pltpu.VMEM(s, jnp.float32) if pin else jax.ShapeDtypeStruct(s, jnp.float32) for s in shapes
        ],
        in_specs=in_specs,
        out_specs=[VMEM] * len(shapes),
        scratch_shapes=[pltpu.VMEM(s, jnp.float32) for s in scratch],
        compiler_params=PARAMS,
        cost_estimate=pl.CostEstimate(flops=flops, bytes_accessed=nbytes, transcendentals=0),
    )
    return (lambda *a: outs(*a)[0]) if single else outs


def apply_stencil(layer, below, above, pot):
    near = below[0] + above[0]
    far = below[1] + above[1]
    rows = layer.shape[0]
    near = near + (pltpu.roll(layer, 1, 0) + pltpu.roll(layer, rows - 1, 0))
    far = far + (pltpu.roll(layer, 2, 0) + pltpu.roll(layer, rows - 2, 0))
    near = near + (pltpu.roll(layer, 1, 1) + pltpu.roll(layer, LANES - 1, 1))
    far = far + (pltpu.roll(layer, 2, 1) + pltpu.roll(layer, LANES - 2, 1))
    return (3.75 + pot) * layer - NEAR * near + FAR * far


def stencil_layers(layers, pot_ref):
    for z in range(len(layers) - 4):
        c = z + 2
        yield z, apply_stencil(
            layers[c], (layers[c - 1], layers[c - 2]), (layers[c + 1], layers[c + 2]), pot_ref[z]
        )


def prior_kernel(field_ref, near_ref, wrapped_ref, pot_ref, out_ref):
    upper = lax.axis_index("zl") == 1

    def step(n, carry):
        near = [near_ref[n, z] for z in range(2)]
        wrapped = [wrapped_ref[n, z] for z in range(2)]
        low = [jnp.where(upper, near[z], wrapped[z]) for z in range(2)]
        high = [jnp.where(upper, wrapped[z], near[z]) for z in range(2)]
        layers = low + [field_ref[n, z] for z in range(field_ref.shape[1])] + high
        for z, value in stencil_layers(layers, pot_ref):
            out_ref[n, z] = value
        return carry

    lax.fori_loop(0, field_ref.shape[0], step, 0)


def put(packed_ref, slot, z, layer, nz):
    rows = nz * layer.shape[0] // NORB
    per_layer = NORB // nz
    for part in range(per_layer):
        packed_ref[z * per_layer + part, slot * rows : (slot + 1) * rows, :] = layer[
            part * rows : (part + 1) * rows
        ]


def inner_kernel(
    prior_ref, field_ref, pot_ref, step_ref,
    packed_ref, near_ref, far_ref, copy_ref, inner_ref, steps_ref,
):
    nprior, nz, nx, _ = prior_ref.shape
    nblk = field_ref.shape[0]
    upper = lax.axis_index("zl") == 1
    for n in range(nprior):
        for z in range(nz):
            put(packed_ref, n, z, prior_ref[n, z], nz)
        for z in range(2):
            top, bottom = prior_ref[n, nz - 2 + z], prior_ref[n, z]
            near_ref[n, z] = jnp.where(upper, bottom, top)
            far_ref[n, z] = jnp.where(upper, top, bottom)
    zero = jnp.zeros((nx, LANES), jnp.float32)
    for n in range(nblk):
        layers = [zero, zero] + [field_ref[n, z] for z in range(nz)] + [zero, zero]
        for z, value in stencil_layers(layers, pot_ref):
            inner_ref[n, z] = value
            copy_ref[n, z] = layers[z + 2]
        steps_ref[n] = jnp.full((8, LANES), step_ref[n], jnp.float32)


def outer_kernel(prior_ref, field_ref, inner_ref, steps_ref, low_ref, high_ref, out_ref, packed_ref):
    nblk, nz, nx, _ = field_ref.shape
    rows = nz * nx // NORB
    nprior = prior_ref.shape[1] // rows
    for dest in range(NORB):
        packed_ref[dest, : nprior * rows, :] = prior_ref[dest]
    for n in range(nblk):
        edge = {
            0: FAR * low_ref[n, 0] - NEAR * low_ref[n, 1],
            1: FAR * low_ref[n, 1],
            nz - 2: FAR * high_ref[n, 0],
            nz - 1: FAR * high_ref[n, 1] - NEAR * high_ref[n, 0],
        }
        step = jnp.broadcast_to(steps_ref[n, 0:1], (nx, LANES))
        for z in range(nz):
            value = inner_ref[n, z] + edge[z]
            out_ref[n, z] = value
            put(packed_ref, nprior + n, z, field_ref[n, z] - step * value, nz)


def split_cells(cells_ref, prior_ref, trial_ref):
    count, split = prior_ref.shape[0] // NORB, trial_ref.shape[0] // NORB
    for s in range(NORB):
        prior_ref[s * count : (s + 1) * count, :] = cells_ref[s, :count, :]
        trial_ref[s * split : (s + 1) * split, :] = cells_ref[s, count:, :]


def make_coef_kernel(nprior, nblk, rows):
    def kernel(cells_ref, out_ref, prior_ref, trial_ref):
        split_cells(cells_ref, prior_ref, trial_ref)
        total = jnp.zeros((nprior, nblk), jnp.float32)
        for r in range(rows):
            left = prior_ref[pl.ds(r, nprior, stride=rows), :]
            right = trial_ref[pl.ds(r, nblk, stride=rows), :]
            total += lax.dot_general(
                left, right, (((1,), (1,)), ((), ())),
                precision=HIGHEST, preferred_element_type=jnp.float32,
            )
        out_ref[...] = total

    return kernel


def make_proj_kernel(nprior, nblk, rows):
    def kernel(coef_ref, cells_ref, out_ref, prior_ref, trial_ref):
        split_cells(cells_ref, prior_ref, trial_ref)
        coef_t = coef_ref[...].T
        for r in range(rows):
            left = prior_ref[pl.ds(r, nprior, stride=rows), :]
            removed = jnp.dot(
                coef_t, left, precision=HIGHEST, preferred_element_type=jnp.float32
            )
            out_ref[pl.ds(r, nblk, stride=rows), :] = (
                trial_ref[pl.ds(r, nblk, stride=rows), :] - removed
            )

    return kernel


def square_kernel(proj_ref, out_ref):
    count = 4
    rows = proj_ref.shape[1] // count
    value = proj_ref[0]
    total = value * value
    for s in range(1, proj_ref.shape[0]):
        value = proj_ref[s]
        total = total + value * value
    zero = jnp.zeros((out_ref.shape[1] - count, LANES), jnp.float32)
    sums = [
        jnp.sum(total[n * rows : (n + 1) * rows], axis=0, keepdims=True) for n in range(count)
    ]
    sums = jnp.concatenate(sums + [zero], axis=0)
    for s in range(out_ref.shape[0]):
        out_ref[s] = sums


def make_scale_kernel(ncells):
    def kernel(proj_ref, parts_ref, out_ref):
        count = out_ref.shape[0]
        rows = proj_ref.shape[1] // count
        total = parts_ref[0]
        for s in range(1, parts_ref.shape[0]):
            total = total + parts_ref[s]
        sqnorm = jnp.sum(total, axis=1, keepdims=True) / ncells
        scale = lax.rsqrt(sqnorm + NORM_EPS)
        for n in range(count):
            factor = jnp.broadcast_to(scale[n : n + 1], (rows, LANES))
            for s in range(proj_ref.shape[0]):
                out_ref[n, s * rows : (s + 1) * rows, :] = (
                    proj_ref[s, n * rows : (n + 1) * rows, :] * factor
                )

    return kernel


def exchange(value, axes):
    return lax.all_to_all(value, axes, 0, 0, tiled=True)


def repeat(value, count):
    return jnp.broadcast_to(value[None], (count,) + value.shape)


def edges(fields):
    return fields[:, -2:], fields[:, :2]


def halos(sides):
    return lax.ppermute(sides[0], GRID, FORWARD), lax.ppermute(sides[1], GRID, BACKWARD)


def on_device(prior, block, potential, step_len):
    nprior_loc, nz, nx, ny = prior.shape
    nblk_loc = block.shape[0]
    nprior, nblk = nprior_loc * NORB, nblk_loc * NORB
    cells = nz * nx * ny
    ncells = cells * NGRID
    rows = nz * nx // NORB
    size = 4 * cells

    blow, bhigh = halos(edges(block))
    prior_rows, near, wrapped, field, inner, steps = call(
        inner_kernel,
        [
            (NORB, nprior_loc * rows, LANES),
            (nprior_loc, 2, nx, ny),
            (nprior_loc, 2, nx, ny),
            block.shape,
            block.shape,
            (nblk_loc, 8, LANES),
        ],
        [VMEM] * 3 + [SMEM],
        20 * nblk_loc * cells,
        (2 * nprior_loc + 4 * nblk_loc) * size,
    )(prior, block, potential, step_len)
    hblock, packed = call(
        outer_kernel,
        [block.shape, (NORB, (nprior_loc + nblk_loc) * rows, LANES)],
        [VMEM] * 6,
        4 * nblk_loc * cells,
        (2 * nprior_loc + 4 * nblk_loc) * size,
    )(prior_rows, field, inner, steps, blow, bhigh)
    moved = exchange(packed, ORB)

    moved, wrapped = lax.optimization_barrier((moved, wrapped))
    coef_bytes = 4 * nprior * nblk
    gemm = 2 * nprior * nblk * rows * LANES
    apart = [(nprior * rows, LANES), (nblk * rows, LANES)]
    partial = call(
        make_coef_kernel(nprior, nblk, rows),
        (nprior, nblk),
        [VMEM],
        gemm,
        8 * coef_bytes,
        scratch=apart,
    )(moved)
    moved, wrapped = lax.optimization_barrier((moved, wrapped))
    coef_bytes = 4 * nprior * nblk
    gemm = 2 * nprior * nblk * rows * LANES
    partial, prior_cells, trial_cells = call(
        make_coef_kernel(nprior, nblk, rows),
        [(nprior, nblk), (nprior * rows, LANES), (nblk * rows, LANES)],
        [VMEM],
        gemm,
        16 * coef_bytes,
    )(moved)
    first = 16
    near = lax.ppermute(near, "zl", SWAP)
    share = jnp.sum(exchange(partial.reshape(first, nprior // first, nblk), ("x", "y")), axis=0)
    share, near = lax.optimization_barrier((share, near))
    share = jnp.sum(exchange(repeat(share, 16), ("zh", "core", "zl")), axis=0) / ncells
    share, wrapped = lax.optimization_barrier((share, wrapped))
    wrapped = lax.ppermute(wrapped, "zl", SWAP)
    coeff = exchange(repeat(share, first), ("x", "y")).reshape(nprior, nblk)

    proj = call(
        make_proj_kernel(nprior, nblk, rows),
        (nblk * rows, LANES),
        [VMEM] * 2,
        gemm,
        10 * coef_bytes,
        scratch=apart,
    )(coeff, moved)
    proj, wrapped = lax.optimization_barrier((proj, wrapped))
    wrapped = lax.ppermute(wrapped, GRID, ALONG)
    back = exchange(proj.reshape(NORB, nblk_loc * rows, LANES), ORB)
    hprior = call(
        prior_kernel, prior.shape, [VMEM] * 4, 20 * nprior_loc * cells, 3 * nprior_loc * size
    )(prior, near, wrapped, potential)
    squares = call(
        square_kernel, (NGRID, 8, LANES), [VMEM], 2 * nblk_loc * cells, nblk_loc * size, pin=True
    )(back)
    totals = exchange(squares, GRID)
    ortho = call(
        make_scale_kernel(ncells),
        (nblk_loc, nz * nx, ny),
        [VMEM] * 2,
        nblk_loc * cells,
        2 * nblk_loc * size,
    )(back, totals)
    return hprior, hblock, ortho.reshape(block.shape)


def solution(mesh):
    fine = Mesh(mesh.devices.reshape(4, 4, 2, 4, 2), ORB + GRID)
    fields = P(ORB, GRID, None, None)
    in_specs = (fields, fields, P(GRID, None, None), P(ORB))
    return jax.shard_map(
        on_device, mesh=fine, in_specs=in_specs, out_specs=(fields,) * 3, check_vma=False
    )
```

```python
import jax
import jax.numpy as jnp
from jax import lax
from jax.experimental import pallas as pl
from jax.experimental.pallas import tpu as pltpu
from jax.sharding import Mesh, PartitionSpec as P

NORM_EPS = 1e-06
NEAR = 2.0 / 3.0
FAR = 1.0 / 24.0
ORB = ("x", "zh", "core")
GRID = ("y", "zl")
NORB = 32
NGRID = 8
LANES = 128
FORWARD = [(i, (i + 1) % NGRID) for i in range(NGRID)]
BACKWARD = [(target, source) for source, target in FORWARD]
SWAP = [(0, 1), (1, 0)]
ALONG = [(i, (i + (NGRID - 2 if i % 2 else 2)) % NGRID) for i in range(NGRID)]
HIGHEST = lax.Precision.HIGHEST
VMEM = pl.BlockSpec(memory_space=pltpu.VMEM)
SMEM = pl.BlockSpec(memory_space=pltpu.SMEM)
PARAMS = pltpu.CompilerParams(vmem_limit_bytes=16 * 1024 * 1024)


def call(kernel, out_shape, in_specs, flops, nbytes, pin=False, scratch=()):
    single = isinstance(out_shape[0], int)
    shapes = [out_shape] if single else list(out_shape)
    outs = pl.pallas_call(
        kernel,
        out_shape=[
            pltpu.VMEM(s, jnp.float32) if pin else jax.ShapeDtypeStruct(s, jnp.float32) for s in shapes
        ],
        in_specs=in_specs,
        out_specs=[VMEM] * len(shapes),
        scratch_shapes=[pltpu.VMEM(s, jnp.float32) for s in scratch],
        compiler_params=PARAMS,
        cost_estimate=pl.CostEstimate(flops=flops, bytes_accessed=nbytes, transcendentals=0),
    )
    return (lambda *a: outs(*a)[0]) if single else outs


def apply_stencil(layer, below, above, pot):
    near = below[0] + above[0]
    far = below[1] + above[1]
    rows = layer.shape[0]
    near = near + (pltpu.roll(layer, 1, 0) + pltpu.roll(layer, rows - 1, 0))
    far = far + (pltpu.roll(layer, 2, 0) + pltpu.roll(layer, rows - 2, 0))
    near = near + (pltpu.roll(layer, 1, 1) + pltpu.roll(layer, LANES - 1, 1))
    far = far + (pltpu.roll(layer, 2, 1) + pltpu.roll(layer, LANES - 2, 1))
    return (3.75 + pot) * layer - NEAR * near + FAR * far


def stencil_layers(layers, pot_ref):
    for z in range(len(layers) - 4):
        c = z + 2
        yield z, apply_stencil(
            layers[c], (layers[c - 1], layers[c - 2]), (layers[c + 1], layers[c + 2]), pot_ref[z]
        )


def prior_kernel(field_ref, near_ref, wrapped_ref, pot_ref, out_ref):
    upper = lax.axis_index("zl") == 1

    def step(n, carry):
        near = [near_ref[n, z] for z in range(2)]
        wrapped = [wrapped_ref[n, z] for z in range(2)]
        low = [jnp.where(upper, near[z], wrapped[z]) for z in range(2)]
        high = [jnp.where(upper, wrapped[z], near[z]) for z in range(2)]
        layers = low + [field_ref[n, z] for z in range(field_ref.shape[1])] + high
        for z, value in stencil_layers(layers, pot_ref):
            out_ref[n, z] = value
        return carry

    lax.fori_loop(0, field_ref.shape[0], step, 0)


def put(packed_ref, slot, z, layer, nz):
    rows = nz * layer.shape[0] // NORB
    per_layer = NORB // nz
    for part in range(per_layer):
        packed_ref[z * per_layer + part, slot * rows : (slot + 1) * rows, :] = layer[
            part * rows : (part + 1) * rows
        ]


def inner_kernel(
    prior_ref, field_ref, pot_ref, step_ref,
    packed_ref, near_ref, far_ref, copy_ref, inner_ref, steps_ref,
):
    nprior, nz, nx, _ = prior_ref.shape
    nblk = field_ref.shape[0]
    upper = lax.axis_index("zl") == 1
    for n in range(nprior):
        for z in range(nz):
            put(packed_ref, n, z, prior_ref[n, z], nz)
        for z in range(2):
            top, bottom = prior_ref[n, nz - 2 + z], prior_ref[n, z]
            near_ref[n, z] = jnp.where(upper, bottom, top)
            far_ref[n, z] = jnp.where(upper, top, bottom)
    zero = jnp.zeros((nx, LANES), jnp.float32)
    for n in range(nblk):
        layers = [zero, zero] + [field_ref[n, z] for z in range(nz)] + [zero, zero]
        for z, value in stencil_layers(layers, pot_ref):
            inner_ref[n, z] = value
            copy_ref[n, z] = layers[z + 2]
        steps_ref[n] = jnp.full((8, LANES), step_ref[n], jnp.float32)


def outer_kernel(prior_ref, field_ref, inner_ref, steps_ref, low_ref, high_ref, out_ref, packed_ref):
    nblk, nz, nx, _ = field_ref.shape
    rows = nz * nx // NORB
    nprior = prior_ref.shape[1] // rows
    for dest in range(NORB):
        packed_ref[dest, : nprior * rows, :] = prior_ref[dest]
    for n in range(nblk):
        edge = {
            0: FAR * low_ref[n, 0] - NEAR * low_ref[n, 1],
            1: FAR * low_ref[n, 1],
            nz - 2: FAR * high_ref[n, 0],
            nz - 1: FAR * high_ref[n, 1] - NEAR * high_ref[n, 0],
        }
        step = jnp.broadcast_to(steps_ref[n, 0:1], (nx, LANES))
        for z in range(nz):
            value = inner_ref[n, z] + edge[z]
            out_ref[n, z] = value
            put(packed_ref, nprior + n, z, field_ref[n, z] - step * value, nz)


def split_cells(cells_ref, prior_ref, trial_ref):
    count, split = prior_ref.shape[0] // NORB, trial_ref.shape[0] // NORB
    for s in range(NORB):
        prior_ref[s * count : (s + 1) * count, :] = cells_ref[s, :count, :]
        trial_ref[s * split : (s + 1) * split, :] = cells_ref[s, count:, :]


def make_coef_kernel(nprior, nblk, rows):
    def kernel(cells_ref, out_ref, prior_ref, trial_ref):
        split_cells(cells_ref, prior_ref, trial_ref)
        total = jnp.zeros((nprior, nblk), jnp.float32)
        for r in range(rows):
            left = prior_ref[pl.ds(r, nprior, stride=rows), :]
            right = trial_ref[pl.ds(r, nblk, stride=rows), :]
            total += lax.dot_general(
                left, right, (((1,), (1,)), ((), ())),
                precision=HIGHEST, preferred_element_type=jnp.float32,
            )
        out_ref[...] = total

    return kernel


def make_proj_kernel(nprior, nblk, rows):
    def kernel(coef_ref, cells_ref, out_ref, prior_ref, trial_ref):
        split_cells(cells_ref, prior_ref, trial_ref)
        coef_t = coef_ref[...].T
        for r in range(0, rows, 2):
            pair = [prior_ref[pl.ds(r + k, nprior, stride=rows), :] for k in range(2)]
            removed = jnp.dot(
                coef_t,
                jnp.concatenate(pair, axis=1),
                precision=HIGHEST,
                preferred_element_type=jnp.float32,
            )
            for k in range(2):
                out_ref[pl.ds(r + k, nblk, stride=rows), :] = (
                    trial_ref[pl.ds(r + k, nblk, stride=rows), :]
                    - removed[:, k * LANES : (k + 1) * LANES]
                )

    return kernel


def square_kernel(proj_ref, out_ref):
    count = 4
    rows = proj_ref.shape[1] // count
    value = proj_ref[0]
    total = value * value
    for s in range(1, proj_ref.shape[0]):
        value = proj_ref[s]
        total = total + value * value
    zero = jnp.zeros((out_ref.shape[1] - count, LANES), jnp.float32)
    sums = [
        jnp.sum(total[n * rows : (n + 1) * rows], axis=0, keepdims=True) for n in range(count)
    ]
    sums = jnp.concatenate(sums + [zero], axis=0)
    for s in range(out_ref.shape[0]):
        out_ref[s] = sums


def make_scale_kernel(ncells):
    def kernel(proj_ref, parts_ref, out_ref):
        count = out_ref.shape[0]
        rows = proj_ref.shape[1] // count
        total = parts_ref[0]
        for s in range(1, parts_ref.shape[0]):
            total = total + parts_ref[s]
        sqnorm = jnp.sum(total, axis=1, keepdims=True) / ncells
        scale = lax.rsqrt(sqnorm + NORM_EPS)
        for n in range(count):
            factor = jnp.broadcast_to(scale[n : n + 1], (rows, LANES))
            for s in range(proj_ref.shape[0]):
                out_ref[n, s * rows : (s + 1) * rows, :] = (
                    proj_ref[s, n * rows : (n + 1) * rows, :] * factor
                )

    return kernel


def exchange(value, axes):
    return lax.all_to_all(value, axes, 0, 0, tiled=True)


def repeat(value, count):
    return jnp.broadcast_to(value[None], (count,) + value.shape)


def edges(fields):
    return fields[:, -2:], fields[:, :2]


def halos(sides):
    return lax.ppermute(sides[0], GRID, FORWARD), lax.ppermute(sides[1], GRID, BACKWARD)


def on_device(prior, block, potential, step_len):
    nprior_loc, nz, nx, ny = prior.shape
    nblk_loc = block.shape[0]
    nprior, nblk = nprior_loc * NORB, nblk_loc * NORB
    cells = nz * nx * ny
    ncells = cells * NGRID
    rows = nz * nx // NORB
    size = 4 * cells

    blow, bhigh = halos(edges(block))
    prior_rows, near, wrapped, field, inner, steps = call(
        inner_kernel,
        [
            (NORB, nprior_loc * rows, LANES),
            (nprior_loc, 2, nx, ny),
            (nprior_loc, 2, nx, ny),
            block.shape,
            block.shape,
            (nblk_loc, 8, LANES),
        ],
        [VMEM] * 3 + [SMEM],
        20 * nblk_loc * cells,
        (2 * nprior_loc + 4 * nblk_loc) * size,
    )(prior, block, potential, step_len)
    hblock, packed = call(
        outer_kernel,
        [block.shape, (NORB, (nprior_loc + nblk_loc) * rows, LANES)],
        [VMEM] * 6,
        4 * nblk_loc * cells,
        (2 * nprior_loc + 4 * nblk_loc) * size,
    )(prior_rows, field, inner, steps, blow, bhigh)
    moved = exchange(packed, ORB)

    moved, wrapped = lax.optimization_barrier((moved, wrapped))
    coef_bytes = 4 * nprior * nblk
    gemm = 2 * nprior * nblk * rows * LANES
    apart = [(nprior * rows, LANES), (nblk * rows, LANES)]
    partial = call(
        make_coef_kernel(nprior, nblk, rows),
        (nprior, nblk),
        [VMEM],
        gemm,
        8 * coef_bytes,
        scratch=apart,
    )(moved)
    moved, wrapped = lax.optimization_barrier((moved, wrapped))
    coef_bytes = 4 * nprior * nblk
    gemm = 2 * nprior * nblk * rows * LANES
    partial, prior_cells, trial_cells = call(
        make_coef_kernel(nprior, nblk, rows),
        [(nprior, nblk), (nprior * rows, LANES), (nblk * rows, LANES)],
        [VMEM],
        gemm,
        16 * coef_bytes,
    )(moved)
    first = 16
    near = lax.ppermute(near, "zl", SWAP)
    share = jnp.sum(exchange(partial.reshape(first, nprior // first, nblk), ("x", "y")), axis=0)
    share, near, wrapped = lax.optimization_barrier((share, near, wrapped))
    wrapped = lax.ppermute(wrapped, "zl", SWAP)
    share = jnp.sum(exchange(repeat(share, 16), ("zh", "core", "zl")), axis=0) / ncells
    coeff = exchange(repeat(share, first), ("x", "y")).reshape(nprior, nblk)

    proj = call(
        make_proj_kernel(nprior, nblk, rows),
        (nblk * rows, LANES),
        [VMEM] * 2,
        gemm,
        10 * coef_bytes,
        scratch=apart,
    )(coeff, moved)
    proj, wrapped = lax.optimization_barrier((proj, wrapped))
    wrapped = lax.ppermute(wrapped, GRID, ALONG)
    back = exchange(proj.reshape(NORB, nblk_loc * rows, LANES), ORB)
    hprior = call(
        prior_kernel, prior.shape, [VMEM] * 4, 20 * nprior_loc * cells, 3 * nprior_loc * size
    )(prior, near, wrapped, potential)
    squares = call(
        square_kernel, (NGRID, 8, LANES), [VMEM], 2 * nblk_loc * cells, nblk_loc * size, pin=True
    )(back)
    totals = exchange(squares, GRID)
    ortho = call(
        make_scale_kernel(ncells),
        (nblk_loc, nz * nx, ny),
        [VMEM] * 2,
        nblk_loc * cells,
        2 * nblk_loc * size,
    )(back, totals)
    return hprior, hblock, ortho.reshape(block.shape)


def solution(mesh):
    fine = Mesh(mesh.devices.reshape(4, 4, 2, 4, 2), ORB + GRID)
    fields = P(ORB, GRID, None, None)
    in_specs = (fields, fields, P(GRID, None, None), P(ORB))
    return jax.shard_map(
        on_device, mesh=fine, in_specs=in_specs, out_specs=(fields,) * 3, check_vma=False
    )
```

```python
import jax
import jax.numpy as jnp
from jax import lax
from jax.experimental import pallas as pl
from jax.experimental.pallas import tpu as pltpu
from jax.sharding import Mesh, PartitionSpec as P

NORM_EPS = 1e-06
NEAR = 2.0 / 3.0
FAR = 1.0 / 24.0
ORB = ("x", "zh", "core")
GRID = ("y", "zl")
NORB = 32
NGRID = 8
LANES = 128
FORWARD = [(i, (i + 1) % NGRID) for i in range(NGRID)]
BACKWARD = [(target, source) for source, target in FORWARD]
SWAP = [(0, 1), (1, 0)]
ALONG = [(i, (i + (NGRID - 2 if i % 2 else 2)) % NGRID) for i in range(NGRID)]
HIGHEST = lax.Precision.HIGHEST
VMEM = pl.BlockSpec(memory_space=pltpu.VMEM)
SMEM = pl.BlockSpec(memory_space=pltpu.SMEM)
PARAMS = pltpu.CompilerParams(vmem_limit_bytes=16 * 1024 * 1024)


def call(kernel, out_shape, in_specs, flops, nbytes, pin=False, scratch=()):
    single = isinstance(out_shape[0], int)
    shapes = [out_shape] if single else list(out_shape)
    outs = pl.pallas_call(
        kernel,
        out_shape=[
            pltpu.VMEM(s, jnp.float32) if pin else jax.ShapeDtypeStruct(s, jnp.float32) for s in shapes
        ],
        in_specs=in_specs,
        out_specs=[VMEM] * len(shapes),
        scratch_shapes=[pltpu.VMEM(s, jnp.float32) for s in scratch],
        compiler_params=PARAMS,
        cost_estimate=pl.CostEstimate(flops=flops, bytes_accessed=nbytes, transcendentals=0),
    )
    return (lambda *a: outs(*a)[0]) if single else outs


def apply_stencil(layer, below, above, pot):
    near = below[0] + above[0]
    far = below[1] + above[1]
    rows = layer.shape[0]
    near = near + (pltpu.roll(layer, 1, 0) + pltpu.roll(layer, rows - 1, 0))
    far = far + (pltpu.roll(layer, 2, 0) + pltpu.roll(layer, rows - 2, 0))
    near = near + (pltpu.roll(layer, 1, 1) + pltpu.roll(layer, LANES - 1, 1))
    far = far + (pltpu.roll(layer, 2, 1) + pltpu.roll(layer, LANES - 2, 1))
    return (3.75 + pot) * layer - NEAR * near + FAR * far


def stencil_layers(layers, pot_ref):
    for z in range(len(layers) - 4):
        c = z + 2
        yield z, apply_stencil(
            layers[c], (layers[c - 1], layers[c - 2]), (layers[c + 1], layers[c + 2]), pot_ref[z]
        )


def prior_kernel(field_ref, near_ref, wrapped_ref, pot_ref, out_ref):
    upper = lax.axis_index("zl") == 1

    def step(n, carry):
        near = [near_ref[n, z] for z in range(2)]
        wrapped = [wrapped_ref[n, z] for z in range(2)]
        low = [jnp.where(upper, near[z], wrapped[z]) for z in range(2)]
        high = [jnp.where(upper, wrapped[z], near[z]) for z in range(2)]
        layers = low + [field_ref[n, z] for z in range(field_ref.shape[1])] + high
        for z, value in stencil_layers(layers, pot_ref):
            out_ref[n, z] = value
        return carry

    lax.fori_loop(0, field_ref.shape[0], step, 0)


def put(packed_ref, slot, z, layer, nz):
    rows = nz * layer.shape[0] // NORB
    per_layer = NORB // nz
    for part in range(per_layer):
        packed_ref[z * per_layer + part, slot * rows : (slot + 1) * rows, :] = layer[
            part * rows : (part + 1) * rows
        ]


def inner_kernel(
    prior_ref, field_ref, pot_ref, step_ref,
    packed_ref, near_ref, far_ref, copy_ref, inner_ref, steps_ref,
):
    nprior, nz, nx, _ = prior_ref.shape
    nblk = field_ref.shape[0]
    upper = lax.axis_index("zl") == 1
    for n in range(nprior):
        for z in range(nz):
            put(packed_ref, n, z, prior_ref[n, z], nz)
        for z in range(2):
            top, bottom = prior_ref[n, nz - 2 + z], prior_ref[n, z]
            near_ref[n, z] = jnp.where(upper, bottom, top)
            far_ref[n, z] = jnp.where(upper, top, bottom)
    zero = jnp.zeros((nx, LANES), jnp.float32)
    for n in range(nblk):
        layers = [zero, zero] + [field_ref[n, z] for z in range(nz)] + [zero, zero]
        for z, value in stencil_layers(layers, pot_ref):
            inner_ref[n, z] = value
            copy_ref[n, z] = layers[z + 2]
        steps_ref[n] = jnp.full((8, LANES), step_ref[n], jnp.float32)


def outer_kernel(
    prior_ref, field_ref, inner_ref, steps_ref, low_ref, high_ref, out_ref, packed_ref, trial_ref, sem
):
    nblk, nz, nx, _ = field_ref.shape
    rows = nz * nx // NORB
    for n in range(nblk):
        edge = {
            0: FAR * low_ref[n, 0] - NEAR * low_ref[n, 1],
            1: FAR * low_ref[n, 1],
            nz - 2: FAR * high_ref[n, 0],
            nz - 1: FAR * high_ref[n, 1] - NEAR * high_ref[n, 0],
        }
        step = jnp.broadcast_to(steps_ref[n, 0:1], (nx, LANES))
        for z in range(nz):
            value = inner_ref[n, z] + edge[z]
            out_ref[n, z] = value
            put(trial_ref, n, z, field_ref[n, z] - step * value, nz)
    width = nblk * rows
    start = packed_ref.shape[1] - width
    copy = pltpu.make_async_copy(trial_ref, packed_ref.at[:, pl.ds(start, width), :], sem)
    copy.start()
    copy.wait()


def split_cells(cells_ref, prior_ref, trial_ref):
    count, split = prior_ref.shape[0] // NORB, trial_ref.shape[0] // NORB
    for s in range(NORB):
        prior_ref[s * count : (s + 1) * count, :] = cells_ref[s, :count, :]
        trial_ref[s * split : (s + 1) * split, :] = cells_ref[s, count:, :]


def make_coef_kernel(nprior, nblk, rows):
    def kernel(cells_ref, out_ref, prior_ref, trial_ref):
        split_cells(cells_ref, prior_ref, trial_ref)
        total = jnp.zeros((nprior, nblk), jnp.float32)
        for r in range(rows):
            left = prior_ref[pl.ds(r, nprior, stride=rows), :]
            right = trial_ref[pl.ds(r, nblk, stride=rows), :]
            total += lax.dot_general(
                left, right, (((1,), (1,)), ((), ())),
                precision=HIGHEST, preferred_element_type=jnp.float32,
            )
        out_ref[...] = total

    return kernel


def make_proj_kernel(nprior, nblk, rows):
    def kernel(coef_ref, cells_ref, out_ref, prior_ref, trial_ref):
        split_cells(cells_ref, prior_ref, trial_ref)
        coef_t = coef_ref[...].T
        for r in range(0, rows, 2):
            pair = [prior_ref[pl.ds(r + k, nprior, stride=rows), :] for k in range(2)]
            removed = jnp.dot(
                coef_t,
                jnp.concatenate(pair, axis=1),
                precision=HIGHEST,
                preferred_element_type=jnp.float32,
            )
            for k in range(2):
                out_ref[pl.ds(r + k, nblk, stride=rows), :] = (
                    trial_ref[pl.ds(r + k, nblk, stride=rows), :]
                    - removed[:, k * LANES : (k + 1) * LANES]
                )

    return kernel


def square_kernel(proj_ref, out_ref):
    count = 4
    rows = proj_ref.shape[1] // count
    value = proj_ref[0]
    total = value * value
    for s in range(1, proj_ref.shape[0]):
        value = proj_ref[s]
        total = total + value * value
    zero = jnp.zeros((out_ref.shape[1] - count, LANES), jnp.float32)
    sums = [
        jnp.sum(total[n * rows : (n + 1) * rows], axis=0, keepdims=True) for n in range(count)
    ]
    sums = jnp.concatenate(sums + [zero], axis=0)
    for s in range(out_ref.shape[0]):
        out_ref[s] = sums


def make_scale_kernel(ncells):
    def kernel(proj_ref, parts_ref, out_ref):
        count = out_ref.shape[0]
        rows = proj_ref.shape[1] // count
        total = parts_ref[0]
        for s in range(1, parts_ref.shape[0]):
            total = total + parts_ref[s]
        sqnorm = jnp.sum(total, axis=1, keepdims=True) / ncells
        scale = lax.rsqrt(sqnorm + NORM_EPS)
        for n in range(count):
            factor = jnp.broadcast_to(scale[n : n + 1], (rows, LANES))
            for s in range(proj_ref.shape[0]):
                out_ref[n, s * rows : (s + 1) * rows, :] = (
                    proj_ref[s, n * rows : (n + 1) * rows, :] * factor
                )

    return kernel


def exchange(value, axes):
    return lax.all_to_all(value, axes, 0, 0, tiled=True)


def repeat(value, count):
    return jnp.broadcast_to(value[None], (count,) + value.shape)


def edges(fields):
    return fields[:, -2:], fields[:, :2]


def halos(sides):
    return lax.ppermute(sides[0], GRID, FORWARD), lax.ppermute(sides[1], GRID, BACKWARD)


def on_device(prior, block, potential, step_len):
    nprior_loc, nz, nx, ny = prior.shape
    nblk_loc = block.shape[0]
    nprior, nblk = nprior_loc * NORB, nblk_loc * NORB
    cells = nz * nx * ny
    ncells = cells * NGRID
    rows = nz * nx // NORB
    size = 4 * cells

    blow, bhigh = halos(edges(block))
    prior_rows, near, wrapped, field, inner, steps = call(
        inner_kernel,
        [
            (NORB, (nprior_loc + nblk_loc) * rows, LANES),
            (nprior_loc, 2, nx, ny),
            (nprior_loc, 2, nx, ny),
            block.shape,
            block.shape,
            (nblk_loc, 8, LANES),
        ],
        [VMEM] * 3 + [SMEM],
        20 * nblk_loc * cells,
        (2 * nprior_loc + 4 * nblk_loc) * size,
    )(prior, block, potential, step_len)
    total_rows = (nprior_loc + nblk_loc) * rows
    hblock, packed = pl.pallas_call(
        outer_kernel,
        out_shape=[
            jax.ShapeDtypeStruct(block.shape, jnp.float32),
            jax.ShapeDtypeStruct((NORB, total_rows, LANES), jnp.float32),
        ],
        in_specs=[pl.BlockSpec(memory_space=pl.ANY)] + [VMEM] * 5,
        out_specs=[VMEM, pl.BlockSpec(memory_space=pl.ANY)],
        scratch_shapes=[
            pltpu.VMEM((NORB, nblk_loc * rows, LANES), jnp.float32),
            pltpu.SemaphoreType.DMA,
        ],
        input_output_aliases={0: 1},
        compiler_params=PARAMS,
        cost_estimate=pl.CostEstimate(
            flops=4 * nblk_loc * cells, bytes_accessed=5 * nblk_loc * size, transcendentals=0
        ),
    )(prior_rows, field, inner, steps, blow, bhigh)
    moved = exchange(packed, ORB)

    moved, wrapped = lax.optimization_barrier((moved, wrapped))
    coef_bytes = 4 * nprior * nblk
    gemm = 2 * nprior * nblk * rows * LANES
    apart = [(nprior * rows, LANES), (nblk * rows, LANES)]
    partial = call(
        make_coef_kernel(nprior, nblk, rows),
        (nprior, nblk),
        [VMEM],
        gemm,
        8 * coef_bytes,
        scratch=apart,
    )(moved)
    moved, wrapped = lax.optimization_barrier((moved, wrapped))
    coef_bytes = 4 * nprior * nblk
    gemm = 2 * nprior * nblk * rows * LANES
    partial, prior_cells, trial_cells = call(
        make_coef_kernel(nprior, nblk, rows),
        [(nprior, nblk), (nprior * rows, LANES), (nblk * rows, LANES)],
        [VMEM],
        gemm,
        16 * coef_bytes,
    )(moved)
    first = 16
    near = lax.ppermute(near, "zl", SWAP)
    share = jnp.sum(exchange(partial.reshape(first, nprior // first, nblk), ("x", "y")), axis=0)
    share, near, wrapped = lax.optimization_barrier((share, near, wrapped))
    wrapped = lax.ppermute(wrapped, "zl", SWAP)
    share = jnp.sum(exchange(repeat(share, 16), ("zh", "core", "zl")), axis=0) / ncells
    coeff = exchange(repeat(share, first), ("x", "y")).reshape(nprior, nblk)

    proj = call(
        make_proj_kernel(nprior, nblk, rows),
        (nblk * rows, LANES),
        [VMEM] * 2,
        gemm,
        10 * coef_bytes,
        scratch=apart,
    )(coeff, moved)
    proj, wrapped = lax.optimization_barrier((proj, wrapped))
    wrapped = lax.ppermute(wrapped, GRID, ALONG)
    back = exchange(proj.reshape(NORB, nblk_loc * rows, LANES), ORB)
    hprior = call(
        prior_kernel, prior.shape, [VMEM] * 4, 20 * nprior_loc * cells, 3 * nprior_loc * size
    )(prior, near, wrapped, potential)
    squares = call(
        square_kernel, (NGRID, 8, LANES), [VMEM], 2 * nblk_loc * cells, nblk_loc * size, pin=True
    )(back)
    totals = exchange(squares, GRID)
    ortho = call(
        make_scale_kernel(ncells),
        (nblk_loc, nz * nx, ny),
        [VMEM] * 2,
        nblk_loc * cells,
        2 * nblk_loc * size,
    )(back, totals)
    return hprior, hblock, ortho.reshape(block.shape)


def solution(mesh):
    fine = Mesh(mesh.devices.reshape(4, 4, 2, 4, 2), ORB + GRID)
    fields = P(ORB, GRID, None, None)
    in_specs = (fields, fields, P(GRID, None, None), P(ORB))
    return jax.shard_map(
        on_device, mesh=fine, in_specs=in_specs, out_specs=(fields,) * 3, check_vma=False
    )
```
